256 devices in a mesh: pts: 64 (over z, x, core), snap: 4 (over y).
Axes of the slice: x: 4, y: 4, z: 8, core: 2. Of those that a mesh axis runs over, the one named last changes fastest.
Arguments:
- snapshots: float32 [262144, 1024], P('pts', 'snap'), may hold values from -6 to 6
- basis: float32 [262144, 128], P('pts'), may hold values from -0.01171875 to 0.01171875
- reg_linear: float32 [129], replicated, may hold values from 0.1 to 1
- reg_quadratic: float32 [8256], P('pts'), may hold values from 0.1 to 1
Outputs:
- coordinates: float32 [128, 1024], P(None, 'snap')
- gram_quad: float32 [8256, 8256], P('pts', 'snap')
- gram_cross: float32 [129, 8256], P(None, 'pts')
- gram_lin: float32 [129, 129], replicated
The draws below stay inside these ranges and needn't reach their ends.
All inputs are finite; a program needn't handle non-finite values.
Results may differ from the reference program's by a relative error of at most 0.00017.
Values sent between devices are 32-bit elements; how exact they have to be, the bound alone decides.
A program may use at most 128 MiB of HBM per device.

```python
import math
import jax
import jax.numpy as jnp
import numpy as np
from jax import lax

R = 128
NPTS = 262144
NSNAP = 1024
NQ = 8256
NQP = 8256
NL = 129


def steps_of(rng, dims, pieces, least, top_value):
    gain = 1.0
    for position, shards_of in pieces:
        steps = jax.random.uniform(jax.random.fold_in(jax.random.fold_in(rng, 6), position), (shards_of,), jnp.float32, least / len(pieces), top_value / len(pieces))
        gain = gain * jnp.repeat(jnp.exp(steps), dims[position] // shards_of).reshape((-1,) + (1,) * (len(dims) - 1 - position))
    return gain


def gaussian(stream_key, extent, deviation, limit, cuts=(), held_as=jnp.bfloat16):
    drawn = jax.random.normal(stream_key, extent, jnp.float32) * deviation
    if len(cuts) > 0:
        drawn = steps_of(stream_key, extent, cuts, -0.22, 0.18) * drawn
    return jnp.clip(drawn, min=-limit, max=limit).astype(held_as)


def setup_inputs(seed: int = 0) -> dict:
    keys = jax.random.split(jax.random.key(seed), 5)
    return {
        "snapshots": gaussian(keys[0], (NPTS, NSNAP), 1.0, 6.0, ((0, 64), (1, 4)), jnp.float32),
        "basis": gaussian(keys[1], (NPTS, R), NPTS ** -0.5, 0.01171875, ((0, 64),), jnp.float32),
        "reg_linear": jnp.clip(jnp.exp(jax.random.uniform(keys[2], (NL,), jnp.float32, math.log(0.1), math.log(1.0))), 0.1, 1.0),
        "reg_quadratic": jnp.clip(jnp.exp(math.log(1.0) - 2.3025851 * jax.random.uniform(keys[3], (NQP,), jnp.float32) ** steps_of(keys[3], (NQP,), ((0, 64),), -0.2, 0.2)), 0.1, 1.0),
    }


def pair_rows(coords):
    first, second = np.triu_indices(coords.shape[0])
    return coords[jnp.asarray(first.astype(np.int32))] * coords[jnp.asarray(second.astype(np.int32))]


def inner(left, right):
    return lax.dot_general(left, right, (((1,), (1,)), ((), ())), precision=lax.Precision.HIGHEST, preferred_element_type=jnp.float32)


def reference(snapshots, basis, reg_linear, reg_quadratic):
    coordinates = lax.dot_general(basis, snapshots, (((0,), (0,)), ((), ())), precision=lax.Precision.HIGHEST, preferred_element_type=jnp.float32)
    count = coordinates.shape[1]
    quad = pair_rows(coordinates)
    quad = jnp.concatenate([quad, jnp.zeros((NQP - NQ, count), jnp.float32)], 0)
    linear = jnp.concatenate([coordinates, jnp.ones((1, count), jnp.float32)], 0)
    gram_quad = inner(quad, quad) / count + jnp.diag(reg_quadratic)
    gram_cross = inner(linear, quad) / count
    gram_lin = inner(linear, linear) / count + jnp.diag(reg_linear)
    return coordinates, gram_quad, gram_cross, gram_lin
```

```python
import functools

import jax
import jax.numpy as jnp
import numpy as np
from jax import lax
from jax.experimental import pallas as pl
from jax.experimental.pallas import tpu as pltpu
from jax.sharding import PartitionSpec as P

R = 128
MESH = pl.DeviceIdType.MESH
CHUNKS = 8
NZ, NX, NC, NY = 8, 4, 2, 4
XY = [(dx, dy) for dy in range(NY) for dx in range(NX) if dx or dy]


def split(value):
    high = value.astype(jnp.bfloat16)
    low = (value - high.astype(jnp.float32)).astype(jnp.bfloat16)
    return high, low


def dot_rows(left, right):
    return lax.dot_general(left, right, (((0,), (0,)), ((), ())), preferred_element_type=jnp.float32)


def gather_kernel(basis_hbm, snaps_hbm, out_hbm, basis, snaps, part, peer, half, from_x, from_z, full,
                  in_sem, c_send, c_recv, x_send, x_recv, z_send, z_recv, xy_send, xy_recv, f_send, f_recv, out_sem):
    pts, y = lax.axis_index("pts"), lax.axis_index("snap")
    z, x, c = pts // (NX * NC), (pts // NC) % NX, pts % NC

    def device(z_of, x_of, c_of, y_of):
        return ((z_of * NX + x_of) * NC + c_of, y_of)

    sibling = device(z, x, 1 - c, y)
    x_peers = [device(z, (x + k) % NX, c, y) for k in range(1, NX)]
    z_peers = [device((z + k) % NZ, x, c, y) for k in range(1, NZ)]
    xy_peers = [device(z, (x + dx) % NX, c, (y + dy) % NY) for dx, dy in XY]

    barrier = pltpu.get_barrier_semaphore()
    greeted = [sibling] + z_peers + xy_peers
    for peer_id in greeted:
        pl.semaphore_signal(barrier, inc=1, device_id=peer_id, device_id_type=MESH)

    rows = basis.shape[1]
    loads = []
    for k in range(CHUNKS):
        for j, (src, dst) in enumerate(((basis_hbm, basis), (snaps_hbm, snaps))):
            load = pltpu.make_async_copy(src.at[pl.ds(k * rows, rows)], dst.at[k], in_sem.at[k, j])
            load.start()
            loads.append(load)
    for k in range(CHUNKS):
        loads[2 * k].wait()
        loads[2 * k + 1].wait()
        b_high, b_low = split(basis[k])
        s_high, s_low = split(snaps[k])
        both = dot_rows(jnp.concatenate([b_high, b_low], axis=1), s_high)
        term = both[:R] + both[R:] + dot_rows(b_high, s_low)
        for h in range(NC):
            if k == 0:
                part[h] = term[:, h * R:(h + 1) * R]
            else:
                part[h] += term[:, h * R:(h + 1) * R]
    pl.semaphore_wait(barrier, len(greeted))

    copy = pltpu.make_async_remote_copy(part.at[1 - c], peer, c_send, c_recv, device_id=sibling, device_id_type=MESH)
    copy.start()
    copy.wait()
    half[...] = (part[c] + peer[...]).reshape(half.shape)

    copies = []
    for k in range(1, NX):
        copy = pltpu.make_async_remote_copy(half.at[(x + k) % NX], from_x.at[k - 1], x_send.at[k - 1], x_recv.at[k - 1],
                                            device_id=x_peers[k - 1], device_id_type=MESH)
        copy.start()
        copies.append(copy)
    for copy in copies:
        copy.wait()
    from_z[z] = half[x] + from_x[0] + from_x[1] + from_x[2]

    copies = []
    for k in range(1, NZ):
        copy = pltpu.make_async_remote_copy(from_z.at[z], from_z.at[z], z_send.at[k - 1], z_recv.at[k - 1],
                                            device_id=z_peers[k - 1], device_id_type=MESH)
        copy.start()
        copies.append(copy)
    for copy in copies:
        copy.wait()
    total = from_z[0]
    for k in range(1, NZ):
        total += from_z[k]
    full[2 * y + c, x] = total

    copies = []
    for n, peer_id in enumerate(xy_peers):
        copy = pltpu.make_async_remote_copy(full.at[2 * y + c, x], full.at[2 * y + c, x], xy_send.at[n], xy_recv.at[n],
                                            device_id=peer_id, device_id_type=MESH)
        copy.start()
        copies.append(copy)
    handed = []
    for dy in range(NY):
        for n, (_, step) in enumerate(XY):
            if step == dy:
                copies[n].wait_recv()
        y_from = (y - dy + NY) % NY
        copy = pltpu.make_async_remote_copy(full.at[2 * y_from + c], full.at[2 * y_from + c], f_send.at[dy], f_recv.at[dy],
                                            device_id=sibling, device_id_type=MESH)
        copy.start()
        handed.append(copy)
    for copy in handed:
        copy.wait_recv()
    copy = pltpu.make_async_copy(full, out_hbm, out_sem)
    copy.start()
    for copy_out in copies + handed:
        copy_out.wait_send()
    copy.wait()


def gather_call(basis, snapshots):
    points, width = snapshots.shape
    rows = points // CHUNKS
    dma = pltpu.SemaphoreType.DMA
    block = (NX, R // NX, R)
    return pl.pallas_call(
        gather_kernel,
        out_shape=jax.ShapeDtypeStruct((NC * NY,) + block, jnp.float32),
        in_specs=[pl.BlockSpec(memory_space=pl.ANY)] * 2,
        out_specs=pl.BlockSpec(memory_space=pl.ANY),
        scratch_shapes=[
            pltpu.VMEM((CHUNKS, rows, R), jnp.float32),
            pltpu.VMEM((CHUNKS, rows, width), jnp.float32),
            pltpu.VMEM((NC, R, R), jnp.float32),
            pltpu.VMEM((R, R), jnp.float32),
            pltpu.VMEM(block, jnp.float32),
            pltpu.VMEM((NX - 1,) + block[1:], jnp.float32),
            pltpu.VMEM((NZ,) + block[1:], jnp.float32),
            pltpu.VMEM((NC * NY,) + block, jnp.float32),
            dma((CHUNKS, 2)),
            dma, dma,
            dma((NX - 1,)), dma((NX - 1,)),
            dma((NZ - 1,)), dma((NZ - 1,)),
            dma((len(XY),)), dma((len(XY),)),
            dma((NY,)), dma((NY,)),
            dma,
        ],
        compiler_params=pltpu.CompilerParams(collective_id=0, has_side_effects=True, vmem_limit_bytes=48 << 20),
        name="project_and_gather",
    )(basis, snapshots)


def pair_table(width):
    return np.stack(np.triu_indices(width), 0).astype(np.int32)


def pair_rows(coords, pairs):
    return jnp.take(coords, pairs[0], axis=0) * jnp.take(coords, pairs[1], axis=0)


def inner(left, right):
    return lax.dot_general(left, right, (((1,), (1,)), ((), ())), precision=lax.Precision.HIGH,
                           preferred_element_type=jnp.float32)


def shards(snapshots, basis, reg_linear, reg_quadratic):
    blocks = gather_call(basis, snapshots).reshape(NC * NY, R, R)
    every = blocks.transpose(1, 0, 2).reshape(R, NC * NY * R)
    group = lax.axis_index("snap")
    local_coords = lax.dynamic_slice_in_dim(every, group * NC * R, NC * R, 1)
    total = every.shape[1]
    scale = 1.0 / total
    row_count = reg_quadratic.shape[0]
    quad_count = row_count * lax.axis_size("pts")
    table = jnp.asarray(pair_table(R))
    row_start = lax.axis_index("pts") * row_count
    col_count = quad_count // lax.axis_size("snap")
    col_start = group * col_count
    row_feats = pair_rows(every, lax.dynamic_slice_in_dim(table, row_start, row_count, 1))
    col_feats = pair_rows(every, lax.dynamic_slice_in_dim(table, col_start, col_count, 1))
    block = inner(row_feats, col_feats)
    row_ids = row_start + jnp.arange(row_count, dtype=jnp.int32)
    col_ids = col_start + jnp.arange(col_count, dtype=jnp.int32)
    on_diag = row_ids[:, None] == col_ids[None, :]
    gram_quad = block * scale + jnp.where(on_diag, reg_quadratic[:, None], 0.0)
    linear = jnp.concatenate([every, jnp.ones((1, total), jnp.float32)], 0)
    gram_cross = inner(linear, row_feats) * scale
    gram_lin = inner(linear, linear) * scale + jnp.diag(reg_linear)
    return (local_coords, gram_quad, gram_cross, gram_lin)


def solution(mesh):
    placed = (P("pts", "snap"), P("pts", None), P(), P("pts"))
    return jax.shard_map(
        shards,
        mesh=mesh,
        in_specs=placed,
        out_specs=(P(None, "snap"), P("pts", "snap"), P(None, "pts"), P()),
        check_vma=False,
    )
```

```python
import functools

import jax
import jax.numpy as jnp
from jax import lax
from jax.experimental import pallas as pl
from jax.experimental.pallas import tpu as pltpu
from jax.sharding import PartitionSpec as P

R = 128
MESH = pl.DeviceIdType.MESH
CHUNKS = 8
STEP = 16
TILE = 256
NZ, NX, NC, NY = 8, 4, 2, 4
XY = [(dx, dy) for dy in range(NY) for dx in range(NX) if dx or dy]


def split(value):
    high = value.astype(jnp.bfloat16)
    low = (value - high.astype(jnp.float32)).astype(jnp.bfloat16)
    return high, low


def dot_rows(left, right):
    return lax.dot_general(left, right, (((0,), (0,)), ((), ())), preferred_element_type=jnp.float32)


def gather_kernel(basis_hbm, snaps_hbm, out_hbm, basis, snaps, part, peer, half, from_x, from_z, full,
                  in_sem, c_send, c_recv, x_send, x_recv, z_send, z_recv, xy_send, xy_recv, f_send, f_recv, out_sem):
    pts, y = lax.axis_index("pts"), lax.axis_index("snap")
    z, x, c = pts // (NX * NC), (pts // NC) % NX, pts % NC

    def device(z_of, x_of, c_of, y_of):
        return ((z_of * NX + x_of) * NC + c_of, y_of)

    sibling = device(z, x, 1 - c, y)
    x_peers = [device(z, (x + k) % NX, c, y) for k in range(1, NX)]
    z_peers = [device((z + k) % NZ, x, c, y) for k in range(1, NZ)]
    xy_peers = [device(z, (x + dx) % NX, c, (y + dy) % NY) for dx, dy in XY]

    barrier = pltpu.get_barrier_semaphore()
    greeted = [sibling] + z_peers + xy_peers
    for peer_id in greeted:
        pl.semaphore_signal(barrier, inc=1, device_id=peer_id, device_id_type=MESH)

    rows = basis.shape[1]
    quarter = half.shape[1]
    loads = []
    for k in range(CHUNKS):
        for j, (src, dst) in enumerate(((basis_hbm, basis), (snaps_hbm, snaps))):
            load = pltpu.make_async_copy(src.at[pl.ds(k * rows, rows)], dst.at[k], in_sem.at[k, j])
            load.start()
            loads.append(load)
    for k in range(CHUNKS):
        loads[2 * k].wait()
        loads[2 * k + 1].wait()
        b_high, b_low = split(basis[k])
        s_high, s_low = split(snaps[k])
        both = dot_rows(jnp.concatenate([b_high, b_low], axis=1), s_high)
        term = both[:R] + both[R:] + dot_rows(b_high, s_low)
        for h in range(NC):
            if k == 0:
                part[h] = term[:, h * R:(h + 1) * R]
            else:
                part[h] += term[:, h * R:(h + 1) * R]
    pl.semaphore_wait(barrier, len(greeted))

    copy = pltpu.make_async_remote_copy(part.at[1 - c], peer, c_send, c_recv, device_id=sibling, device_id_type=MESH)
    copy.start()
    copy.wait()
    half[...] = (part[c] + peer[...]).reshape(half.shape)

    copies = []
    for k in range(1, NX):
        copy = pltpu.make_async_remote_copy(half.at[(x + k) % NX], from_x.at[k - 1], x_send.at[k - 1], x_recv.at[k - 1],
                                            device_id=x_peers[k - 1], device_id_type=MESH)
        copy.start()
        copies.append(copy)
    for copy in copies:
        copy.wait()
    from_z[z] = half[x] + from_x[0] + from_x[1] + from_x[2]

    copies = []
    for k in range(1, NZ):
        copy = pltpu.make_async_remote_copy(from_z.at[z], from_z.at[z], z_send.at[k - 1], z_recv.at[k - 1],
                                            device_id=z_peers[k - 1], device_id_type=MESH)
        copy.start()
        copies.append(copy)
    for copy in copies:
        copy.wait()
    total = from_z[0]
    for k in range(1, NZ):
        total += from_z[k]
    mine = full.at[2 * y + c, pl.ds(pl.multiple_of(x * quarter, quarter), quarter)]
    mine[...] = total

    copies = []
    for n, peer_id in enumerate(xy_peers):
        copy = pltpu.make_async_remote_copy(mine, mine, xy_send.at[n], xy_recv.at[n],
                                            device_id=peer_id, device_id_type=MESH)
        copy.start()
        copies.append(copy)
    handed = []
    for dy in range(NY):
        for n, (_, step) in enumerate(XY):
            if step == dy:
                copies[n].wait_recv()
        y_from = (y - dy + NY) % NY
        copy = pltpu.make_async_remote_copy(full.at[2 * y_from + c], full.at[2 * y_from + c], f_send.at[dy], f_recv.at[dy],
                                            device_id=sibling, device_id_type=MESH)
        copy.start()
        handed.append(copy)
    for copy in handed:
        copy.wait_recv()
    copy = pltpu.make_async_copy(full, out_hbm.at[:, pl.ds(0, R)], out_sem)
    copy.start()
    for copy_out in copies + handed:
        copy_out.wait_send()
    copy.wait()


def gather_call(basis, snapshots):
    points, width = snapshots.shape
    rows = points // CHUNKS
    dma = pltpu.SemaphoreType.DMA
    block = (NX, R // NX, R)
    return pl.pallas_call(
        gather_kernel,
        out_shape=jax.ShapeDtypeStruct((NC * NY, R + STEP, R), jnp.float32),
        in_specs=[pl.BlockSpec(memory_space=pl.ANY)] * 2,
        out_specs=pl.BlockSpec(memory_space=pl.ANY),
        scratch_shapes=[
            pltpu.VMEM((CHUNKS, rows, R), jnp.float32),
            pltpu.VMEM((CHUNKS, rows, width), jnp.float32),
            pltpu.VMEM((NC, R, R), jnp.float32),
            pltpu.VMEM((R, R), jnp.float32),
            pltpu.VMEM(block, jnp.float32),
            pltpu.VMEM((NX - 1,) + block[1:], jnp.float32),
            pltpu.VMEM((NZ,) + block[1:], jnp.float32),
            pltpu.VMEM((NC * NY, R, R), jnp.float32),
            dma((CHUNKS, 2)),
            dma, dma,
            dma((NX - 1,)), dma((NX - 1,)),
            dma((NZ - 1,)), dma((NZ - 1,)),
            dma((len(XY),)), dma((len(XY),)),
            dma((NY,)), dma((NY,)),
            dma,
        ],
        compiler_params=pltpu.CompilerParams(collective_id=0, has_side_effects=True, vmem_limit_bytes=48 << 20),
        name="project_and_gather",
    )(basis, snapshots)


def first_index(pair):
    found = jnp.int32(0)
    for step in (64, 32, 16, 8, 4, 2, 1):
        tried = found + step
        found = jnp.where(pairs_before(tried) <= pair, tried, found)
    return found


def pairs_before(i):
    return R * i - i * (i - 1) // 2


def build_features(coords, feats, start, count):
    first, last = first_index(start), first_index(start + count - 1)

    @pl.loop(first, last + 1)
    def _(i):
        begun = pairs_before(i)
        into = jnp.maximum(begun - start, 0)
        j = i + jnp.maximum(start - begun, 0)
        length = jnp.minimum(R - j, count - into)
        base = coords[:, pl.ds(i, 1), :]

        @pl.loop(0, (length + STEP - 1) // STEP)
        def _(m):
            feats[:, pl.ds(into + m * STEP, STEP), :] = base * coords[:, pl.ds(j + m * STEP, STEP), :]


def lanes(blocks):
    return jnp.concatenate([blocks[t] for t in range(blocks.shape[0])], axis=1)


def gram_kernel(coords, reg_lin, reg_quad, local_out, quad_out, cross_out, lin_out, row_feats, col_feats, rows_split, lin_split):
    pts, y = lax.axis_index("pts"), lax.axis_index("snap")
    row_count, col_count = quad_out.shape
    padded = rows_split.shape[1]
    total = rows_split.shape[2]
    scale = 1.0 / total
    row_start, col_start = pts * row_count, y * col_count
    for h in range(NC):
        local_out[:, h * R:(h + 1) * R] = coords[NC * y + h, :R, :]
    build_features(coords, row_feats, row_start, row_count)
    build_features(coords, col_feats, col_start, col_count)

    for t in range(coords.shape[0]):
        high, low = split(row_feats[t, :padded, :])
        rows_split[0, :, t * R:(t + 1) * R] = high
        rows_split[1, :, t * R:(t + 1) * R] = low
        extra = jnp.where(lax.broadcasted_iota(jnp.int32, (padded - R, R), 0) == 0, 1.0, 0.0)
        high, low = split(jnp.concatenate([coords[t, :R, :], extra], axis=0))
        lin_split[0, :, t * R:(t + 1) * R] = high
        lin_split[1, :, t * R:(t + 1) * R] = low

    def product(left, right_high, right_low):
        dims = (((1,), (1,)), ((), ()))
        both = lax.dot_general(left[...].reshape(2 * padded, total), right_high, dims, preferred_element_type=jnp.float32)
        return both[:padded] + both[padded:] + lax.dot_general(left[0], right_low, dims, preferred_element_type=jnp.float32)

    def regs_down(reg):
        shape = (padded, reg.shape[1])
        on = lax.broadcasted_iota(jnp.int32, shape, 0) == lax.broadcasted_iota(jnp.int32, shape, 1)
        return on, jnp.sum(jnp.where(on, jnp.broadcast_to(reg[...], shape), 0.0), axis=1, keepdims=True)

    on, reg_column = regs_down(reg_lin)
    size = lin_out.shape[0]
    cross_out[...] = (product(lin_split, rows_split[0], rows_split[1]) * scale)[:size, :row_count]
    gram = (product(lin_split, lin_split[0], lin_split[1]) * scale)[:size, :size]
    lin_out[...] = gram + jnp.where(on[:size, :size], reg_column[:size], 0.0)

    _, reg_column = regs_down(reg_quad)

    def tile(begin, width, kept):
        feats = [split(col_feats[t, pl.ds(begin, width), :]) for t in range(coords.shape[0])]
        gram = product(rows_split, jnp.concatenate([f[0] for f in feats], axis=1), jnp.concatenate([f[1] for f in feats], axis=1)) * scale
        shape = gram.shape
        on_diag = (lax.broadcasted_iota(jnp.int32, shape, 1) - lax.broadcasted_iota(jnp.int32, shape, 0)
                   == row_start - col_start - begin)
        gram += jnp.where(on_diag, reg_column, 0.0)
        quad_out[:, pl.ds(begin, kept)] = gram[:row_count, :kept]

    whole = col_count // TILE

    @pl.loop(0, whole)
    def _(n):
        tile(pl.multiple_of(n * TILE, TILE), TILE, TILE)

    if col_count > whole * TILE:
        tile(whole * TILE, R, col_count - whole * TILE)


def up(value, multiple):
    return -(-value // multiple) * multiple


def gram_call(coords, reg_linear, reg_quadratic, quad_count):
    chunks, _, width = coords.shape
    total = chunks * width
    row_count, col_count = reg_quadratic.shape[0], quad_count // NY
    size = reg_linear.shape[0]
    padded = up(row_count, 16)
    vmem = pl.BlockSpec(memory_space=pltpu.VMEM)
    f32 = jnp.float32
    return pl.pallas_call(
        gram_kernel,
        out_shape=(
            jax.ShapeDtypeStruct((R, NC * R), f32),
            jax.ShapeDtypeStruct((row_count, col_count), f32),
            jax.ShapeDtypeStruct((size, row_count), f32),
            jax.ShapeDtypeStruct((size, size), f32),
        ),
        in_specs=[vmem] * 3,
        out_specs=(vmem,) * 4,
        scratch_shapes=[
            pltpu.VMEM((chunks, up(row_count, STEP) + STEP, width), f32),
            pltpu.VMEM((chunks, up(col_count, R) + STEP, width), f32),
            pltpu.VMEM((2, padded, total), jnp.bfloat16),
            pltpu.VMEM((2, padded, total), jnp.bfloat16),
        ],
        compiler_params=pltpu.CompilerParams(vmem_limit_bytes=48 << 20),
        name="pair_gram",
    )(coords, reg_linear.reshape(1, -1), reg_quadratic.reshape(1, -1))


def shards(snapshots, basis, reg_linear, reg_quadratic):
    coords = gather_call(basis, snapshots)
    return gram_call(coords, reg_linear, reg_quadratic, reg_quadratic.shape[0] * NZ * NX * NC)


def solution(mesh):
    placed = (P("pts", "snap"), P("pts", None), P(), P("pts"))
    return jax.shard_map(
        shards,
        mesh=mesh,
        in_specs=placed,
        out_specs=(P(None, "snap"), P("pts", "snap"), P(None, "pts"), P()),
        check_vma=False,
    )
```

```python
import functools

import jax
import jax.numpy as jnp
from jax import lax
from jax.experimental import pallas as pl
from jax.experimental.pallas import tpu as pltpu
from jax.sharding import PartitionSpec as P

R = 128
MESH = pl.DeviceIdType.MESH
CHUNKS = 8
STEP = 16
TILE = 256
NZ, NX, NC, NY = 8, 4, 2, 4
XY = [(dx, dy) for dy in range(NY) for dx in range(NX) if dx or dy]
XY.sort(key=lambda d: min(d[0], NX - d[0]) + min(d[1], NY - d[1]))


def far_first(size):
    return sorted(range(1, size), key=lambda k: -min(k, size - k))


def split(value):
    high = value.astype(jnp.bfloat16)
    low = (value - high.astype(jnp.float32)).astype(jnp.bfloat16)
    return high, low


def dot_rows(left, right):
    return lax.dot_general(left, right, (((0,), (0,)), ((), ())), preferred_element_type=jnp.float32)


def gather_kernel(basis_hbm, snaps_hbm, out, basis, snaps, part, peer, half, from_x, from_z, block,
                  in_sem, c_send, c_recv, x_send, x_recv, z_send, z_recv, xy_send, xy_recv, b_send, b_recv,
                  f_send, f_recv, own_sem):
    pts, y = lax.axis_index("pts"), lax.axis_index("snap")
    z, x, c = pts // (NX * NC), (pts // NC) % NX, pts % NC
    rows, quarter = basis.shape[1], half.shape[1]

    def device(z_of, x_of, c_of, y_of):
        return ((z_of * NX + x_of) * NC + c_of, y_of)

    sibling = device(z, x, 1 - c, y)
    across = device(z, (x + NX // 2) % NX, 1 - c, (y + NY // 2) % NY)
    z_peers = [device((z + k) % NZ, x, c, y) for k in range(1, NZ)]
    xy_peers = [device(z, (x + dx) % NX, c, (y + dy) % NY) for dx, dy in XY]
    sends = []

    loads = []
    for k in range(CHUNKS):
        for j, (src, dst) in enumerate(((basis_hbm, basis), (snaps_hbm, snaps))):
            load = pltpu.make_async_copy(src.at[pl.ds(k * rows, rows)], dst.at[k], in_sem.at[k, j])
            load.start()
            loads.append(load)

    barrier = pltpu.get_barrier_semaphore()
    greeted = [sibling, across] + z_peers + xy_peers
    for peer_id in greeted:
        pl.semaphore_signal(barrier, inc=1, device_id=peer_id, device_id_type=MESH)

    def send(src, dst, send_sem, recv_sem, target):
        copy = pltpu.make_async_remote_copy(src, dst, send_sem, recv_sem, device_id=target, device_id_type=MESH)
        copy.start()
        sends.append(copy)
        return copy

    for k in range(CHUNKS):
        loads[2 * k].wait()
        loads[2 * k + 1].wait()
        b_high, b_low = split(basis[k])
        s_high, s_low = split(snaps[k])
        both = dot_rows(jnp.concatenate([b_high, b_low], axis=1), s_high)
        term = both[:R] + both[R:] + dot_rows(b_high, s_low)
        for h in range(NC):
            if k == 0:
                part[h] = term[:, h * R:(h + 1) * R]
            else:
                part[h] += term[:, h * R:(h + 1) * R]
    pl.semaphore_wait(barrier, len(greeted))

    send(part.at[1 - c], peer, c_send, c_recv, sibling).wait_recv()
    half[...] = (part[c] + peer[...]).reshape(half.shape)

    copies = [send(half.at[(x + k) % NX], from_x.at[k - 1], x_send.at[k - 1], x_recv.at[k - 1],
                   device(z, (x + k) % NX, c, y)) for k in far_first(NX)]
    for copy in copies:
        copy.wait_recv()
    from_z[z] = half[x] + from_x[0] + from_x[1] + from_x[2]

    copies = [send(from_z.at[z], from_z.at[z], z_send.at[k - 1], z_recv.at[k - 1], z_peers[k - 1]) for k in far_first(NZ)]
    for copy in copies:
        copy.wait_recv()
    total = from_z[0]
    for k in range(1, NZ):
        total += from_z[k]
    block[...] = total

    def place(x_of, y_of):
        return out.at[NC * y_of + c, pl.ds(pl.multiple_of(x_of * quarter, quarter), quarter)]

    mine = place(x, y)
    far = len(XY) - 1
    copies = {far: send(block, mine, xy_send.at[far], xy_recv.at[far], xy_peers[far])}
    both_cores = send(block, mine, b_send, b_recv, across)
    for n in range(far - 1, -1, -1):
        copies[n] = send(block, mine, xy_send.at[n], xy_recv.at[n], xy_peers[n])
    handed = [send(block, mine, f_send.at[far], f_recv.at[far], sibling)]
    own = pltpu.make_async_copy(block, mine, own_sem)
    own.start()
    for n in range(far):
        copies[n].wait_recv()
        dx, dy = XY[n]
        came = place((x - dx + NX) % NX, (y - dy + NY) % NY)
        handed.append(send(came, came, f_send.at[n], f_recv.at[n], sibling))
    copies[far].wait_recv()
    both_cores.wait_recv()
    for copy in handed:
        copy.wait_recv()
    for copy in sends:
        copy.wait_send()
    own.wait()


def gather_call(basis, snapshots):
    points, width = snapshots.shape
    rows = points // CHUNKS
    dma = pltpu.SemaphoreType.DMA
    block = (NX, R // NX, R)
    return pl.pallas_call(
        gather_kernel,
        out_shape=jax.ShapeDtypeStruct((NC * NY, R + STEP, R), jnp.float32),
        in_specs=[pl.BlockSpec(memory_space=pl.ANY)] * 2,
        out_specs=pl.BlockSpec(memory_space=pl.ANY),
        scratch_shapes=[
            pltpu.VMEM((CHUNKS, rows, R), jnp.float32),
            pltpu.VMEM((CHUNKS, rows, width), jnp.float32),
            pltpu.VMEM((NC, R, R), jnp.float32),
            pltpu.VMEM((R, R), jnp.float32),
            pltpu.VMEM(block, jnp.float32),
            pltpu.VMEM((NX - 1,) + block[1:], jnp.float32),
            pltpu.VMEM((NZ,) + block[1:], jnp.float32),
            pltpu.VMEM(block[1:], jnp.float32),
            dma((CHUNKS, 2)),
            dma, dma,
            dma((NX - 1,)), dma((NX - 1,)),
            dma((NZ - 1,)), dma((NZ - 1,)),
            dma((len(XY),)), dma((len(XY),)),
            dma, dma,
            dma((len(XY),)), dma((len(XY),)),
            dma,
        ],
        compiler_params=pltpu.CompilerParams(collective_id=0, has_side_effects=True, vmem_limit_bytes=52 << 20),
        name="project_and_gather",
    )(basis, snapshots)


def first_index(pair):
    found = jnp.int32(0)
    for step in (64, 32, 16, 8, 4, 2, 1):
        tried = found + step
        found = jnp.where(pairs_before(tried) <= pair, tried, found)
    return found


def pairs_before(i):
    return R * i - i * (i - 1) // 2


def build_features(coords, feats, start, count):
    first, last = first_index(start), first_index(start + count - 1)

    @pl.loop(first, last + 1)
    def _(i):
        begun = pairs_before(i)
        into = jnp.maximum(begun - start, 0)
        j = i + jnp.maximum(start - begun, 0)
        length = jnp.minimum(R - j, count - into)
        base = coords[:, pl.ds(i, 1), :]

        @pl.loop(0, (length + STEP - 1) // STEP)
        def _(m):
            feats[:, pl.ds(into + m * STEP, STEP), :] = base * coords[:, pl.ds(j + m * STEP, STEP), :]


def lanes(blocks):
    return jnp.concatenate([blocks[t] for t in range(blocks.shape[0])], axis=1)


def gram_kernel(coords, reg_lin, reg_quad, local_out, quad_out, cross_out, lin_out, row_feats, col_feats, rows_split, lin_split):
    pts, y = lax.axis_index("pts"), lax.axis_index("snap")
    row_count, col_count = quad_out.shape
    padded = rows_split.shape[1]
    total = rows_split.shape[2]
    scale = 1.0 / total
    row_start, col_start = pts * row_count, y * col_count
    for h in range(NC):
        local_out[:, h * R:(h + 1) * R] = coords[NC * y + h, :R, :]
    build_features(coords, row_feats, row_start, row_count)
    build_features(coords, col_feats, col_start, col_count)

    for t in range(coords.shape[0]):
        high, low = split(row_feats[t, :padded, :])
        rows_split[0, :, t * R:(t + 1) * R] = high
        rows_split[1, :, t * R:(t + 1) * R] = low
        extra = jnp.where(lax.broadcasted_iota(jnp.int32, (padded - R, R), 0) == 0, 1.0, 0.0)
        high, low = split(jnp.concatenate([coords[t, :R, :], extra], axis=0))
        lin_split[0, :, t * R:(t + 1) * R] = high
        lin_split[1, :, t * R:(t + 1) * R] = low

    def product(left, right_high, right_low):
        dims = (((1,), (1,)), ((), ()))
        both = lax.dot_general(left[...].reshape(2 * padded, total), right_high, dims, preferred_element_type=jnp.float32)
        return both[:padded] + both[padded:] + lax.dot_general(left[0], right_low, dims, preferred_element_type=jnp.float32)

    def regs_down(reg):
        shape = (padded, reg.shape[1])
        on = lax.broadcasted_iota(jnp.int32, shape, 0) == lax.broadcasted_iota(jnp.int32, shape, 1)
        return on, jnp.sum(jnp.where(on, jnp.broadcast_to(reg[...], shape), 0.0), axis=1, keepdims=True)

    on, reg_column = regs_down(reg_lin)
    size = lin_out.shape[0]
    cross_out[...] = (product(lin_split, rows_split[0], rows_split[1]) * scale)[:size, :row_count]
    gram = (product(lin_split, lin_split[0], lin_split[1]) * scale)[:size, :size]
    lin_out[...] = gram + jnp.where(on[:size, :size], reg_column[:size], 0.0)

    _, reg_column = regs_down(reg_quad)

    def tile(begin, width, kept):
        feats = [split(col_feats[t, pl.ds(begin, width), :]) for t in range(coords.shape[0])]
        gram = product(rows_split, jnp.concatenate([f[0] for f in feats], axis=1), jnp.concatenate([f[1] for f in feats], axis=1)) * scale
        shape = gram.shape
        on_diag = (lax.broadcasted_iota(jnp.int32, shape, 1) - lax.broadcasted_iota(jnp.int32, shape, 0)
                   == row_start - col_start - begin)
        gram += jnp.where(on_diag, reg_column, 0.0)
        quad_out[:, pl.ds(begin, kept)] = gram[:row_count, :kept]

    whole = col_count // TILE

    @pl.loop(0, whole, unroll=8)
    def _(n):
        tile(pl.multiple_of(n * TILE, TILE), TILE, TILE)

    if col_count > whole * TILE:
        tile(whole * TILE, R, col_count - whole * TILE)


def up(value, multiple):
    return -(-value // multiple) * multiple


def gram_call(coords, reg_linear, reg_quadratic, quad_count):
    chunks, _, width = coords.shape
    total = chunks * width
    row_count, col_count = reg_quadratic.shape[0], quad_count // NY
    size = reg_linear.shape[0]
    padded = up(row_count, 16)
    vmem = pl.BlockSpec(memory_space=pltpu.VMEM)
    f32 = jnp.float32
    return pl.pallas_call(
        gram_kernel,
        out_shape=(
            jax.ShapeDtypeStruct((R, NC * R), f32),
            jax.ShapeDtypeStruct((row_count, col_count), f32),
            jax.ShapeDtypeStruct((size, row_count), f32),
            jax.ShapeDtypeStruct((size, size), f32),
        ),
        in_specs=[vmem] * 3,
        out_specs=(vmem,) * 4,
        scratch_shapes=[
            pltpu.VMEM((chunks, up(row_count, STEP) + STEP, width), f32),
            pltpu.VMEM((chunks, up(col_count, R) + STEP, width), f32),
            pltpu.VMEM((2, padded, total), jnp.bfloat16),
            pltpu.VMEM((2, padded, total), jnp.bfloat16),
        ],
        compiler_params=pltpu.CompilerParams(vmem_limit_bytes=48 << 20),
        name="pair_gram",
    )(coords, reg_linear.reshape(1, -1), reg_quadratic.reshape(1, -1))


def shards(snapshots, basis, reg_linear, reg_quadratic):
    coords = gather_call(basis, snapshots)
    return gram_call(coords, reg_linear, reg_quadratic, reg_quadratic.shape[0] * NZ * NX * NC)


def solution(mesh):
    placed = (P("pts", "snap"), P("pts", None), P(), P("pts"))
    return jax.shard_map(
        shards,
        mesh=mesh,
        in_specs=placed,
        out_specs=(P(None, "snap"), P("pts", "snap"), P(None, "pts"), P()),
        check_vma=False,
    )
```

```python
import functools

import jax
import jax.numpy as jnp
from jax import lax
from jax.experimental import pallas as pl
from jax.experimental.pallas import tpu as pltpu
from jax.sharding import PartitionSpec as P

R = 128
MESH = pl.DeviceIdType.MESH
CHUNKS = 4
STEP = 16
TILE = 256
NZ, NX, NC, NY = 8, 4, 2, 4
XY = [(dx, dy) for dy in range(NY) for dx in range(NX) if dx or dy]


def hops(step):
    return min(step[0], NX - step[0]) + min(step[1], NY - step[1])


XY.sort(key=hops)


def far_first(size):
    return sorted(range(1, size), key=lambda k: -min(k, size - k))


def split(value):
    high = value.astype(jnp.bfloat16)
    low = (value - high.astype(jnp.float32)).astype(jnp.bfloat16)
    return high, low


def dot_rows(left, right):
    return lax.dot_general(left, right, (((0,), (0,)), ((), ())), preferred_element_type=jnp.float32)


def gather_kernel(basis_hbm, snaps_hbm, out, basis, snaps, part, peer, half, from_x, from_z, block,
                  in_sem, c_send, c_recv, x_send, x_recv, z_send, z_recv, xy_send, xy_recv,
                  f_send, f_recv, own_sem):
    pts, y = lax.axis_index("pts"), lax.axis_index("snap")
    z, x, c = pts // (NX * NC), (pts // NC) % NX, pts % NC
    rows, quarter = basis.shape[1], half.shape[1]

    def device(z_of, x_of, c_of, y_of):
        return ((z_of * NX + x_of) * NC + c_of, y_of)

    sibling = device(z, x, 1 - c, y)
    z_peers = [device((z + k) % NZ, x, c, y) for k in range(1, NZ)]
    xy_peers = [device(z, (x + dx) % NX, c, (y + dy) % NY) for dx, dy in XY]
    sends = []

    loads = []
    for k in range(CHUNKS):
        for j, (src, dst) in enumerate(((basis_hbm, basis), (snaps_hbm, snaps))):
            load = pltpu.make_async_copy(src.at[pl.ds(k * rows, rows)], dst.at[k], in_sem.at[k, j])
            load.start()
            loads.append(load)

    barrier = pltpu.get_barrier_semaphore()
    greeted = [sibling] + z_peers + xy_peers
    for peer_id in greeted:
        pl.semaphore_signal(barrier, inc=1, device_id=peer_id, device_id_type=MESH)

    def send(src, dst, send_sem, recv_sem, target):
        copy = pltpu.make_async_remote_copy(src, dst, send_sem, recv_sem, device_id=target, device_id_type=MESH)
        copy.start()
        sends.append(copy)
        return copy

    for k in range(CHUNKS):
        loads[2 * k].wait()
        loads[2 * k + 1].wait()
        b_high, b_low = split(basis[k])
        s_high, s_low = split(snaps[k])
        both = dot_rows(jnp.concatenate([b_high, b_low], axis=1), s_high)
        term = both[:R] + both[R:] + dot_rows(b_high, s_low)
        for h in range(NC):
            if k == 0:
                part[h] = term[:, h * R:(h + 1) * R]
            else:
                part[h] += term[:, h * R:(h + 1) * R]
    pl.semaphore_wait(barrier, len(greeted))

    send(part.at[1 - c], peer, c_send, c_recv, sibling).wait_recv()
    half[...] = (part[c] + peer[...]).reshape(half.shape)

    copies = [send(half.at[(x + k) % NX], from_x.at[k - 1], x_send.at[k - 1], x_recv.at[k - 1],
                   device(z, (x + k) % NX, c, y)) for k in far_first(NX)]
    for copy in copies:
        copy.wait_recv()
    from_z[z] = half[x] + from_x[0] + from_x[1] + from_x[2]

    copies = [send(from_z.at[z], from_z.at[z], z_send.at[k - 1], z_recv.at[k - 1], z_peers[k - 1]) for k in far_first(NZ)]
    for copy in copies:
        copy.wait_recv()
    total = from_z[0]
    for k in range(1, NZ):
        total += from_z[k]
    block[...] = total

    def place(x_of, y_of):
        return out.at[NC * y_of + c, pl.ds(pl.multiple_of(x_of * quarter, quarter), quarter)]

    mine = place(x, y)
    last = len(XY)
    copies, handed = {}, []
    for n in range(last - 1, -1, -1):
        copies[n] = send(block, mine, xy_send.at[n], xy_recv.at[n], xy_peers[n])
    handed.append(send(block, mine, f_send.at[last], f_recv.at[last], sibling))
    own = pltpu.make_async_copy(block, mine, own_sem)
    own.start()
    for n in range(last):
        copies[n].wait_recv()
        dx, dy = XY[n]
        came = place((x - dx + NX) % NX, (y - dy + NY) % NY)
        handed.append(send(came, came, f_send.at[n], f_recv.at[n], sibling))
    for copy in handed:
        copy.wait_recv()
    for copy in sends:
        copy.wait_send()
    own.wait()


def gather_call(basis, snapshots):
    points, width = snapshots.shape
    rows = points // CHUNKS
    dma = pltpu.SemaphoreType.DMA
    block = (NX, R // NX, R)
    return pl.pallas_call(
        gather_kernel,
        out_shape=jax.ShapeDtypeStruct((NC * NY, R + STEP, R), jnp.float32),
        in_specs=[pl.BlockSpec(memory_space=pl.ANY)] * 2,
        out_specs=pl.BlockSpec(memory_space=pl.ANY),
        scratch_shapes=[
            pltpu.VMEM((CHUNKS, rows, R), jnp.float32),
            pltpu.VMEM((CHUNKS, rows, width), jnp.float32),
            pltpu.VMEM((NC, R, R), jnp.float32),
            pltpu.VMEM((R, R), jnp.float32),
            pltpu.VMEM(block, jnp.float32),
            pltpu.VMEM((NX - 1,) + block[1:], jnp.float32),
            pltpu.VMEM((NZ,) + block[1:], jnp.float32),
            pltpu.VMEM(block[1:], jnp.float32),
            dma((CHUNKS, 2)),
            dma, dma,
            dma((NX - 1,)), dma((NX - 1,)),
            dma((NZ - 1,)), dma((NZ - 1,)),
            dma((len(XY),)), dma((len(XY),)),
            dma((len(XY) + 1,)), dma((len(XY) + 1,)),
            dma,
        ],
        compiler_params=pltpu.CompilerParams(collective_id=0, has_side_effects=True, vmem_limit_bytes=52 << 20),
        name="project_and_gather",
    )(basis, snapshots)


def first_index(pair):
    found = jnp.int32(0)
    for step in (64, 32, 16, 8, 4, 2, 1):
        tried = found + step
        found = jnp.where(pairs_before(tried) <= pair, tried, found)
    return found


def pairs_before(i):
    return R * i - i * (i - 1) // 2


def build_features(coords, feats, start, count):
    first, last = first_index(start), first_index(start + count - 1)

    @pl.loop(first, last + 1)
    def _(i):
        begun = pairs_before(i)
        into = jnp.maximum(begun - start, 0)
        j = i + jnp.maximum(start - begun, 0)
        length = jnp.minimum(R - j, count - into)
        base = coords[:, pl.ds(i, 1), :]

        @pl.loop(0, (length + STEP - 1) // STEP)
        def _(m):
            feats[:, pl.ds(into + m * STEP, STEP), :] = base * coords[:, pl.ds(j + m * STEP, STEP), :]


def lanes(blocks):
    return jnp.concatenate([blocks[t] for t in range(blocks.shape[0])], axis=1)


def gram_kernel(coords, reg_lin, reg_quad, local_out, quad_out, cross_out, lin_out, row_feats, col_feats, rows_split, lin_split):
    pts, y = lax.axis_index("pts"), lax.axis_index("snap")
    row_count, col_count = quad_out.shape
    padded = rows_split.shape[1]
    total = rows_split.shape[2]
    scale = 1.0 / total
    row_start, col_start = pts * row_count, y * col_count
    for h in range(NC):
        local_out[:, h * R:(h + 1) * R] = coords[NC * y + h, :R, :]
    build_features(coords, row_feats, row_start, row_count)
    build_features(coords, col_feats, col_start, col_count)

    for t in range(coords.shape[0]):
        high, low = split(row_feats[t, :padded, :])
        rows_split[0, :, t * R:(t + 1) * R] = high
        rows_split[1, :, t * R:(t + 1) * R] = low
        extra = jnp.where(lax.broadcasted_iota(jnp.int32, (padded - R, R), 0) == 0, 1.0, 0.0)
        high, low = split(jnp.concatenate([coords[t, :R, :], extra], axis=0))
        lin_split[0, :, t * R:(t + 1) * R] = high
        lin_split[1, :, t * R:(t + 1) * R] = low

    def product(left, right_high, right_low):
        dims = (((1,), (1,)), ((), ()))
        both = lax.dot_general(left[...].reshape(2 * padded, total), right_high, dims, preferred_element_type=jnp.float32)
        return both[:padded] + both[padded:] + lax.dot_general(left[0], right_low, dims, preferred_element_type=jnp.float32)

    def regs_down(reg):
        shape = (padded, reg.shape[1])
        on = lax.broadcasted_iota(jnp.int32, shape, 0) == lax.broadcasted_iota(jnp.int32, shape, 1)
        return on, jnp.sum(jnp.where(on, jnp.broadcast_to(reg[...], shape), 0.0), axis=1, keepdims=True)

    on, reg_column = regs_down(reg_lin)
    size = lin_out.shape[0]
    cross_out[...] = (product(lin_split, rows_split[0], rows_split[1]) * scale)[:size, :row_count]
    gram = (product(lin_split, lin_split[0], lin_split[1]) * scale)[:size, :size]
    lin_out[...] = gram + jnp.where(on[:size, :size], reg_column[:size], 0.0)

    _, reg_column = regs_down(reg_quad)

    def tile(begin, width, kept):
        feats = [split(col_feats[t, pl.ds(begin, width), :]) for t in range(coords.shape[0])]
        gram = product(rows_split, jnp.concatenate([f[0] for f in feats], axis=1), jnp.concatenate([f[1] for f in feats], axis=1)) * scale
        shape = gram.shape
        on_diag = (lax.broadcasted_iota(jnp.int32, shape, 1) - lax.broadcasted_iota(jnp.int32, shape, 0)
                   == row_start - col_start - begin)
        gram += jnp.where(on_diag, reg_column, 0.0)
        quad_out[:, pl.ds(begin, kept)] = gram[:row_count, :kept]

    whole = col_count // TILE

    @pl.loop(0, whole, unroll=8)
    def _(n):
        tile(pl.multiple_of(n * TILE, TILE), TILE, TILE)

    if col_count > whole * TILE:
        tile(whole * TILE, R, col_count - whole * TILE)


def up(value, multiple):
    return -(-value // multiple) * multiple


def gram_call(coords, reg_linear, reg_quadratic, quad_count):
    chunks, _, width = coords.shape
    total = chunks * width
    row_count, col_count = reg_quadratic.shape[0], quad_count // NY
    size = reg_linear.shape[0]
    padded = up(row_count, 16)
    vmem = pl.BlockSpec(memory_space=pltpu.VMEM)
    f32 = jnp.float32
    return pl.pallas_call(
        gram_kernel,
        out_shape=(
            jax.ShapeDtypeStruct((R, NC * R), f32),
            jax.ShapeDtypeStruct((row_count, col_count), f32),
            jax.ShapeDtypeStruct((size, row_count), f32),
            jax.ShapeDtypeStruct((size, size), f32),
        ),
        in_specs=[vmem] * 3,
        out_specs=(vmem,) * 4,
        scratch_shapes=[
            pltpu.VMEM((chunks, up(row_count, STEP) + STEP, width), f32),
            pltpu.VMEM((chunks, up(col_count, R) + STEP, width), f32),
            pltpu.VMEM((2, padded, total), jnp.bfloat16),
            pltpu.VMEM((2, padded, total), jnp.bfloat16),
        ],
        compiler_params=pltpu.CompilerParams(vmem_limit_bytes=48 << 20),
        name="pair_gram",
    )(coords, reg_linear.reshape(1, -1), reg_quadratic.reshape(1, -1))


def shards(snapshots, basis, reg_linear, reg_quadratic):
    coords = gather_call(basis, snapshots)
    return gram_call(coords, reg_linear, reg_quadratic, reg_quadratic.shape[0] * NZ * NX * NC)


def solution(mesh):
    placed = (P("pts", "snap"), P("pts", None), P(), P("pts"))
    return jax.shard_map(
        shards,
        mesh=mesh,
        in_specs=placed,
        out_specs=(P(None, "snap"), P("pts", "snap"), P(None, "pts"), P()),
        check_vma=False,
    )
```

```python
import functools

import jax
import jax.numpy as jnp
from jax import lax
from jax.experimental import pallas as pl
from jax.experimental.pallas import tpu as pltpu
from jax.sharding import PartitionSpec as P

R = 128
MESH = pl.DeviceIdType.MESH
CHUNKS = 4
STEP = 16
TILE = 256
NZ, NX, NC, NY = 8, 4, 2, 4
XY = [(dx, dy) for dy in range(NY) for dx in range(NX) if dx or dy]


def hops(step):
    return min(step[0], NX - step[0]) + min(step[1], NY - step[1])


XY.sort(key=hops)
ROW = [(dx, dc) for dx in (2, 1, 3, 0) for dc in range(NC) if dx or dc]


def far_first(size):
    return sorted(range(1, size), key=lambda k: -min(k, size - k))


def split(value):
    high = value.astype(jnp.bfloat16)
    low = (value - high.astype(jnp.float32)).astype(jnp.bfloat16)
    return high, low


def dot_rows(left, right):
    return lax.dot_general(left, right, (((0,), (0,)), ((), ())), preferred_element_type=jnp.float32)


def gather_kernel(basis_hbm, snaps_hbm, out, basis, snaps, part, from_x, from_z, block,
                  in_sem, x_send, x_recv, z_send, z_recv, xy_send, xy_recv,
                  f_send, f_recv, own_sem):
    pts, y = lax.axis_index("pts"), lax.axis_index("snap")
    z, x, c = pts // (NX * NC), (pts // NC) % NX, pts % NC
    rows, quarter = basis.shape[1], part.shape[2]

    def device(z_of, x_of, c_of, y_of):
        return ((z_of * NX + x_of) * NC + c_of, y_of)

    sibling = device(z, x, 1 - c, y)
    z_peers = [device((z + k) % NZ, x, c, y) for k in range(1, NZ)]
    xy_peers = [device(z, (x + dx) % NX, c, (y + dy) % NY) for dx, dy in XY]
    row_peers = [device(z, (x + dx) % NX, (c + dc) % NC, y) for dx, dc in ROW]
    sends = []

    loads = []
    for k in range(CHUNKS):
        for j, (src, dst) in enumerate(((basis_hbm, basis), (snaps_hbm, snaps))):
            load = pltpu.make_async_copy(src.at[pl.ds(k * rows, rows)], dst.at[k], in_sem.at[k, j])
            load.start()
            loads.append(load)

    barrier = pltpu.get_barrier_semaphore()
    greeted = [peer for peer, (_, dc) in zip(row_peers, ROW) if dc] + z_peers + xy_peers
    for peer_id in greeted:
        pl.semaphore_signal(barrier, inc=1, device_id=peer_id, device_id_type=MESH)

    def send(src, dst, send_sem, recv_sem, target):
        copy = pltpu.make_async_remote_copy(src, dst, send_sem, recv_sem, device_id=target, device_id_type=MESH)
        copy.start()
        sends.append(copy)
        return copy

    for k in range(CHUNKS):
        loads[2 * k].wait()
        loads[2 * k + 1].wait()
        b_high, b_low = split(basis[k])
        s_high, s_low = split(snaps[k])
        both = dot_rows(jnp.concatenate([b_high, b_low], axis=1), s_high)
        term = both[:R] + both[R:] + dot_rows(b_high, s_low)
        for h in range(NC):
            if k == 0:
                part[h] = term[:, h * R:(h + 1) * R].reshape(part.shape[1:])
            else:
                part[h] += term[:, h * R:(h + 1) * R].reshape(part.shape[1:])
    pl.semaphore_wait(barrier, len(greeted))

    copies = [send(part.at[(c + dc) % NC, (x + dx) % NX], from_x.at[n], x_send.at[n], x_recv.at[n], row_peers[n])
              for n, (dx, dc) in enumerate(ROW)]
    for copy in copies:
        copy.wait_recv()
    total = part[c, x]
    for n in range(len(ROW)):
        total += from_x[n]
    from_z[z] = total

    copies = [send(from_z.at[z], from_z.at[z], z_send.at[k - 1], z_recv.at[k - 1], z_peers[k - 1]) for k in far_first(NZ)]
    for copy in copies:
        copy.wait_recv()
    total = from_z[0]
    for k in range(1, NZ):
        total += from_z[k]
    block[...] = total

    def place(x_of, y_of):
        return out.at[NC * y_of + c, pl.ds(pl.multiple_of(x_of * quarter, quarter), quarter)]

    mine = place(x, y)
    last = len(XY)
    copies, handed = {}, []
    for n in range(last - 1, -1, -1):
        copies[n] = send(block, mine, xy_send.at[n], xy_recv.at[n], xy_peers[n])
    handed.append(send(block, mine, f_send.at[last], f_recv.at[last], sibling))
    own = pltpu.make_async_copy(block, mine, own_sem)
    own.start()
    for n in range(last):
        copies[n].wait_recv()
        dx, dy = XY[n]
        came = place((x - dx + NX) % NX, (y - dy + NY) % NY)
        handed.append(send(came, came, f_send.at[n], f_recv.at[n], sibling))
    for copy in handed:
        copy.wait_recv()
    for copy in sends:
        copy.wait_send()
    own.wait()


def gather_call(basis, snapshots):
    points, width = snapshots.shape
    rows = points // CHUNKS
    dma = pltpu.SemaphoreType.DMA
    block = (NX, R // NX, R)
    return pl.pallas_call(
        gather_kernel,
        out_shape=jax.ShapeDtypeStruct((NC * NY, R + STEP, R), jnp.float32),
        in_specs=[pl.BlockSpec(memory_space=pl.ANY)] * 2,
        out_specs=pl.BlockSpec(memory_space=pl.ANY),
        scratch_shapes=[
            pltpu.VMEM((CHUNKS, rows, R), jnp.float32),
            pltpu.VMEM((CHUNKS, rows, width), jnp.float32),
            pltpu.VMEM((NC,) + block, jnp.float32),
            pltpu.VMEM((len(ROW),) + block[1:], jnp.float32),
            pltpu.VMEM((NZ,) + block[1:], jnp.float32),
            pltpu.VMEM(block[1:], jnp.float32),
            dma((CHUNKS, 2)),
            dma((len(ROW),)), dma((len(ROW),)),
            dma((NZ - 1,)), dma((NZ - 1,)),
            dma((len(XY),)), dma((len(XY),)),
            dma((len(XY) + 1,)), dma((len(XY) + 1,)),
            dma,
        ],
        compiler_params=pltpu.CompilerParams(collective_id=0, has_side_effects=True, vmem_limit_bytes=52 << 20),
        name="project_and_gather",
    )(basis, snapshots)


def first_index(pair):
    found = jnp.int32(0)
    for step in (64, 32, 16, 8, 4, 2, 1):
        tried = found + step
        found = jnp.where(pairs_before(tried) <= pair, tried, found)
    return found


def pairs_before(i):
    return R * i - i * (i - 1) // 2


def build_features(coords, feats, start, count):
    first, last = first_index(start), first_index(start + count - 1)

    @pl.loop(first, last + 1)
    def _(i):
        begun = pairs_before(i)
        into = jnp.maximum(begun - start, 0)
        j = i + jnp.maximum(start - begun, 0)
        length = jnp.minimum(R - j, count - into)
        base = coords[:, pl.ds(i, 1), :]

        @pl.loop(0, (length + STEP - 1) // STEP)
        def _(m):
            feats[:, pl.ds(into + m * STEP, STEP), :] = base * coords[:, pl.ds(j + m * STEP, STEP), :]


def lanes(blocks):
    return jnp.concatenate([blocks[t] for t in range(blocks.shape[0])], axis=1)


def gram_kernel(coords, reg_lin, reg_quad, local_out, quad_out, cross_out, lin_out, row_feats, col_feats, rows_split, lin_split):
    pts, y = lax.axis_index("pts"), lax.axis_index("snap")
    row_count, col_count = quad_out.shape
    padded = rows_split.shape[1]
    total = rows_split.shape[2]
    scale = 1.0 / total
    row_start, col_start = pts * row_count, y * col_count
    for h in range(NC):
        local_out[:, h * R:(h + 1) * R] = coords[NC * y + h, :R, :]
    build_features(coords, row_feats, row_start, row_count)
    build_features(coords, col_feats, col_start, col_count)

    for t in range(coords.shape[0]):
        high, low = split(row_feats[t, :padded, :])
        rows_split[0, :, t * R:(t + 1) * R] = high
        rows_split[1, :, t * R:(t + 1) * R] = low
        extra = jnp.where(lax.broadcasted_iota(jnp.int32, (padded - R, R), 0) == 0, 1.0, 0.0)
        high, low = split(jnp.concatenate([coords[t, :R, :], extra], axis=0))
        lin_split[0, :, t * R:(t + 1) * R] = high
        lin_split[1, :, t * R:(t + 1) * R] = low

    def product(left, right_high, right_low):
        dims = (((1,), (1,)), ((), ()))
        both = lax.dot_general(left[...].reshape(2 * padded, total), right_high, dims, preferred_element_type=jnp.float32)
        return both[:padded] + both[padded:] + lax.dot_general(left[0], right_low, dims, preferred_element_type=jnp.float32)

    def regs_down(reg):
        shape = (padded, reg.shape[1])
        on = lax.broadcasted_iota(jnp.int32, shape, 0) == lax.broadcasted_iota(jnp.int32, shape, 1)
        return on, jnp.sum(jnp.where(on, jnp.broadcast_to(reg[...], shape), 0.0), axis=1, keepdims=True)

    on, reg_column = regs_down(reg_lin)
    size = lin_out.shape[0]
    cross_out[...] = (product(lin_split, rows_split[0], rows_split[1]) * scale)[:size, :row_count]
    gram = (product(lin_split, lin_split[0], lin_split[1]) * scale)[:size, :size]
    lin_out[...] = gram + jnp.where(on[:size, :size], reg_column[:size], 0.0)

    _, reg_column = regs_down(reg_quad)

    def tile(begin, width, kept):
        feats = [split(col_feats[t, pl.ds(begin, width), :]) for t in range(coords.shape[0])]
        gram = product(rows_split, jnp.concatenate([f[0] for f in feats], axis=1), jnp.concatenate([f[1] for f in feats], axis=1)) * scale
        shape = gram.shape
        on_diag = (lax.broadcasted_iota(jnp.int32, shape, 1) - lax.broadcasted_iota(jnp.int32, shape, 0)
                   == row_start - col_start - begin)
        gram += jnp.where(on_diag, reg_column, 0.0)
        quad_out[:, pl.ds(begin, kept)] = gram[:row_count, :kept]

    whole = col_count // TILE

    @pl.loop(0, whole, unroll=8)
    def _(n):
        tile(pl.multiple_of(n * TILE, TILE), TILE, TILE)

    if col_count > whole * TILE:
        tile(whole * TILE, R, col_count - whole * TILE)


def up(value, multiple):
    return -(-value // multiple) * multiple


def gram_call(coords, reg_linear, reg_quadratic, quad_count):
    chunks, _, width = coords.shape
    total = chunks * width
    row_count, col_count = reg_quadratic.shape[0], quad_count // NY
    size = reg_linear.shape[0]
    padded = up(row_count, 16)
    vmem = pl.BlockSpec(memory_space=pltpu.VMEM)
    f32 = jnp.float32
    return pl.pallas_call(
        gram_kernel,
        out_shape=(
            jax.ShapeDtypeStruct((R, NC * R), f32),
            jax.ShapeDtypeStruct((row_count, col_count), f32),
            jax.ShapeDtypeStruct((size, row_count), f32),
            jax.ShapeDtypeStruct((size, size), f32),
        ),
        in_specs=[vmem] * 3,
        out_specs=(vmem,) * 4,
        scratch_shapes=[
            pltpu.VMEM((chunks, up(row_count, STEP) + STEP, width), f32),
            pltpu.VMEM((chunks, up(col_count, R) + STEP, width), f32),
            pltpu.VMEM((2, padded, total), jnp.bfloat16),
            pltpu.VMEM((2, padded, total), jnp.bfloat16),
        ],
        compiler_params=pltpu.CompilerParams(vmem_limit_bytes=48 << 20),
        name="pair_gram",
    )(coords, reg_linear.reshape(1, -1), reg_quadratic.reshape(1, -1))


def shards(snapshots, basis, reg_linear, reg_quadratic):
    coords = gather_call(basis, snapshots)
    return gram_call(coords, reg_linear, reg_quadratic, reg_quadratic.shape[0] * NZ * NX * NC)


def solution(mesh):
    placed = (P("pts", "snap"), P("pts", None), P(), P("pts"))
    return jax.shard_map(
        shards,
        mesh=mesh,
        in_specs=placed,
        out_specs=(P(None, "snap"), P("pts", "snap"), P(None, "pts"), P()),
        check_vma=False,
    )
```

```python
import functools

import jax
import jax.numpy as jnp
from jax import lax
from jax.experimental import pallas as pl
from jax.experimental.pallas import tpu as pltpu
from jax.sharding import PartitionSpec as P

R = 128
MESH = pl.DeviceIdType.MESH
CHUNKS = 4
STEP = 16
TILE = 256
NZ, NX, NC, NY = 8, 4, 2, 4
XY = [(dx, dy) for dy in range(NY) for dx in range(NX) if dx or dy]


def hops(step):
    return min(step[0], NX - step[0]) + min(step[1], NY - step[1])


XY.sort(key=hops)
ROW = [(dx, dc) for dx in (0, 2, 1, 3) for dc in range(NC) if dx or dc]


def far_first(size):
    return sorted(range(1, size), key=lambda k: -min(k, size - k))


def split(value):
    high = value.astype(jnp.bfloat16)
    low = (value - high.astype(jnp.float32)).astype(jnp.bfloat16)
    return high, low


def dot_rows(left, right):
    return lax.dot_general(left, right, (((0,), (0,)), ((), ())), preferred_element_type=jnp.float32)


def gather_kernel(basis_hbm, snaps_hbm, out, basis, snaps, part, from_x, from_z, block,
                  in_sem, x_send, x_recv, z_send, z_recv, xy_send, xy_recv,
                  f_send, f_recv, own_sem):
    pts, y = lax.axis_index("pts"), lax.axis_index("snap")
    z, x, c = pts // (NX * NC), (pts // NC) % NX, pts % NC
    rows, quarter = basis.shape[1], part.shape[2]

    def device(z_of, x_of, c_of, y_of):
        return ((z_of * NX + x_of) * NC + c_of, y_of)

    sibling = device(z, x, 1 - c, y)
    z_peers = [device((z + k) % NZ, x, c, y) for k in range(1, NZ)]
    xy_peers = [device(z, (x + dx) % NX, c, (y + dy) % NY) for dx, dy in XY]
    row_peers = [device(z, (x + dx) % NX, (c + dc) % NC, y) for dx, dc in ROW]
    sends = []

    loads = []
    for k in range(CHUNKS):
        for j, (src, dst) in enumerate(((basis_hbm, basis), (snaps_hbm, snaps))):
            load = pltpu.make_async_copy(src.at[pl.ds(k * rows, rows)], dst.at[k], in_sem.at[k, j])
            load.start()
            loads.append(load)

    barrier = pltpu.get_barrier_semaphore()
    greeted = [peer for peer, (_, dc) in zip(row_peers, ROW) if dc] + z_peers + xy_peers
    for peer_id in greeted:
        pl.semaphore_signal(barrier, inc=1, device_id=peer_id, device_id_type=MESH)

    def send(src, dst, send_sem, recv_sem, target):
        copy = pltpu.make_async_remote_copy(src, dst, send_sem, recv_sem, device_id=target, device_id_type=MESH)
        copy.start()
        sends.append(copy)
        return copy

    for k in range(CHUNKS):
        loads[2 * k].wait()
        loads[2 * k + 1].wait()
        b_high, b_low = split(basis[k])
        s_high, s_low = split(snaps[k])
        both = dot_rows(jnp.concatenate([b_high, b_low], axis=1), s_high)
        term = both[:R] + both[R:] + dot_rows(b_high, s_low)
        for h in range(NC):
            if k == 0:
                part[h] = term[:, h * R:(h + 1) * R].reshape(part.shape[1:])
            else:
                part[h] += term[:, h * R:(h + 1) * R].reshape(part.shape[1:])
    pl.semaphore_wait(barrier, len(greeted))

    copies = [send(part.at[(c + dc) % NC, (x + dx) % NX], from_x.at[n], x_send.at[n], x_recv.at[n], row_peers[n])
              for n, (dx, dc) in enumerate(ROW)]
    for copy in copies:
        copy.wait_recv()
    total = part[c, x]
    for n in range(len(ROW)):
        total += from_x[n]
    from_z[z] = total

    copies = [send(from_z.at[z], from_z.at[z], z_send.at[k - 1], z_recv.at[k - 1], z_peers[k - 1]) for k in far_first(NZ)]
    for copy in copies:
        copy.wait_recv()
    total = from_z[0]
    for k in range(1, NZ):
        total += from_z[k]
    block[...] = total

    def place(x_of, y_of):
        return out.at[NC * y_of + c, pl.ds(pl.multiple_of(x_of * quarter, quarter), quarter)]

    mine = place(x, y)
    last = len(XY)
    copies, handed = {}, []
    handed.append(send(block, mine, f_send.at[last], f_recv.at[last], sibling))
    for n in range(last - 1, -1, -1):
        copies[n] = send(block, mine, xy_send.at[n], xy_recv.at[n], xy_peers[n])
    own = pltpu.make_async_copy(block, mine, own_sem)
    own.start()
    for n in range(last):
        copies[n].wait_recv()
        dx, dy = XY[n]
        came = place((x - dx + NX) % NX, (y - dy + NY) % NY)
        handed.append(send(came, came, f_send.at[n], f_recv.at[n], sibling))
    for copy in handed:
        copy.wait_recv()
    for copy in sends:
        copy.wait_send()
    own.wait()


def gather_call(basis, snapshots):
    points, width = snapshots.shape
    rows = points // CHUNKS
    dma = pltpu.SemaphoreType.DMA
    block = (NX, R // NX, R)
    return pl.pallas_call(
        gather_kernel,
        out_shape=jax.ShapeDtypeStruct((NC * NY, R + STEP, R), jnp.float32),
        in_specs=[pl.BlockSpec(memory_space=pl.ANY)] * 2,
        out_specs=pl.BlockSpec(memory_space=pl.ANY),
        scratch_shapes=[
            pltpu.VMEM((CHUNKS, rows, R), jnp.float32),
            pltpu.VMEM((CHUNKS, rows, width), jnp.float32),
            pltpu.VMEM((NC,) + block, jnp.float32),
            pltpu.VMEM((len(ROW),) + block[1:], jnp.float32),
            pltpu.VMEM((NZ,) + block[1:], jnp.float32),
            pltpu.VMEM(block[1:], jnp.float32),
            dma((CHUNKS, 2)),
            dma((len(ROW),)), dma((len(ROW),)),
            dma((NZ - 1,)), dma((NZ - 1,)),
            dma((len(XY),)), dma((len(XY),)),
            dma((len(XY) + 1,)), dma((len(XY) + 1,)),
            dma,
        ],
        compiler_params=pltpu.CompilerParams(collective_id=0, has_side_effects=True, vmem_limit_bytes=52 << 20),
        name="project_and_gather",
    )(basis, snapshots)


def first_index(pair):
    found = jnp.int32(0)
    for step in (64, 32, 16, 8, 4, 2, 1):
        tried = found + step
        found = jnp.where(pairs_before(tried) <= pair, tried, found)
    return found


def pairs_before(i):
    return R * i - i * (i - 1) // 2


def build_features(coords, feats, start, count):
    first, last = first_index(start), first_index(start + count - 1)

    @pl.loop(first, last + 1)
    def _(i):
        begun = pairs_before(i)
        into = jnp.maximum(begun - start, 0)
        j = i + jnp.maximum(start - begun, 0)
        length = jnp.minimum(R - j, count - into)
        base = coords[:, pl.ds(i, 1), :]

        @pl.loop(0, (length + STEP - 1) // STEP)
        def _(m):
            feats[:, pl.ds(into + m * STEP, STEP), :] = base * coords[:, pl.ds(j + m * STEP, STEP), :]


def lanes(blocks):
    return jnp.concatenate([blocks[t] for t in range(blocks.shape[0])], axis=1)


def gram_kernel(coords, reg_lin, reg_quad, local_out, quad_out, cross_out, lin_out, row_feats, col_feats, rows_split, lin_split):
    pts, y = lax.axis_index("pts"), lax.axis_index("snap")
    row_count, col_count = quad_out.shape
    padded = rows_split.shape[1]
    total = rows_split.shape[2]
    scale = 1.0 / total
    row_start, col_start = pts * row_count, y * col_count
    for h in range(NC):
        local_out[:, h * R:(h + 1) * R] = coords[NC * y + h, :R, :]
    build_features(coords, row_feats, row_start, row_count)
    build_features(coords, col_feats, col_start, col_count)

    for t in range(coords.shape[0]):
        high, low = split(row_feats[t, :padded, :])
        rows_split[0, :, t * R:(t + 1) * R] = high
        rows_split[1, :, t * R:(t + 1) * R] = low
        extra = jnp.where(lax.broadcasted_iota(jnp.int32, (padded - R, R), 0) == 0, 1.0, 0.0)
        high, low = split(jnp.concatenate([coords[t, :R, :], extra], axis=0))
        lin_split[0, :, t * R:(t + 1) * R] = high
        lin_split[1, :, t * R:(t + 1) * R] = low

    def product(left, right_high, right_low):
        dims = (((1,), (1,)), ((), ()))
        both = lax.dot_general(left[...].reshape(2 * padded, total), right_high, dims, preferred_element_type=jnp.float32)
        return both[:padded] + both[padded:] + lax.dot_general(left[0], right_low, dims, preferred_element_type=jnp.float32)

    def regs_down(reg):
        shape = (padded, reg.shape[1])
        on = lax.broadcasted_iota(jnp.int32, shape, 0) == lax.broadcasted_iota(jnp.int32, shape, 1)
        return on, jnp.sum(jnp.where(on, jnp.broadcast_to(reg[...], shape), 0.0), axis=1, keepdims=True)

    on, reg_column = regs_down(reg_lin)
    size = lin_out.shape[0]
    cross_out[...] = (product(lin_split, rows_split[0], rows_split[1]) * scale)[:size, :row_count]
    gram = (product(lin_split, lin_split[0], lin_split[1]) * scale)[:size, :size]
    lin_out[...] = gram + jnp.where(on[:size, :size], reg_column[:size], 0.0)

    _, reg_column = regs_down(reg_quad)

    def tile(begin, width, kept):
        feats = [split(col_feats[t, pl.ds(begin, width), :]) for t in range(coords.shape[0])]
        gram = product(rows_split, jnp.concatenate([f[0] for f in feats], axis=1), jnp.concatenate([f[1] for f in feats], axis=1)) * scale
        shape = gram.shape
        on_diag = (lax.broadcasted_iota(jnp.int32, shape, 1) - lax.broadcasted_iota(jnp.int32, shape, 0)
                   == row_start - col_start - begin)
        gram += jnp.where(on_diag, reg_column, 0.0)
        quad_out[:, pl.ds(begin, kept)] = gram[:row_count, :kept]

    whole = col_count // TILE

    @pl.loop(0, whole, unroll=8)
    def _(n):
        tile(pl.multiple_of(n * TILE, TILE), TILE, TILE)

    if col_count > whole * TILE:
        tile(whole * TILE, R, col_count - whole * TILE)


def up(value, multiple):
    return -(-value // multiple) * multiple


def gram_call(coords, reg_linear, reg_quadratic, quad_count):
    chunks, _, width = coords.shape
    total = chunks * width
    row_count, col_count = reg_quadratic.shape[0], quad_count // NY
    size = reg_linear.shape[0]
    padded = up(row_count, 16)
    vmem = pl.BlockSpec(memory_space=pltpu.VMEM)
    f32 = jnp.float32
    return pl.pallas_call(
        gram_kernel,
        out_shape=(
            jax.ShapeDtypeStruct((R, NC * R), f32),
            jax.ShapeDtypeStruct((row_count, col_count), f32),
            jax.ShapeDtypeStruct((size, row_count), f32),
            jax.ShapeDtypeStruct((size, size), f32),
        ),
        in_specs=[vmem] * 3,
        out_specs=(vmem,) * 4,
        scratch_shapes=[
            pltpu.VMEM((chunks, up(row_count, STEP) + STEP, width), f32),
            pltpu.VMEM((chunks, up(col_count, R) + STEP, width), f32),
            pltpu.VMEM((2, padded, total), jnp.bfloat16),
            pltpu.VMEM((2, padded, total), jnp.bfloat16),
        ],
        compiler_params=pltpu.CompilerParams(vmem_limit_bytes=48 << 20),
        name="pair_gram",
    )(coords, reg_linear.reshape(1, -1), reg_quadratic.reshape(1, -1))


def shards(snapshots, basis, reg_linear, reg_quadratic):
    coords = gather_call(basis, snapshots)
    return gram_call(coords, reg_linear, reg_quadratic, reg_quadratic.shape[0] * NZ * NX * NC)


def solution(mesh):
    placed = (P("pts", "snap"), P("pts", None), P(), P("pts"))
    return jax.shard_map(
        shards,
        mesh=mesh,
        in_specs=placed,
        out_specs=(P(None, "snap"), P("pts", "snap"), P(None, "pts"), P()),
        check_vma=False,
    )
```

```python
import functools

import jax
import jax.numpy as jnp
from jax import lax
from jax.experimental import pallas as pl
from jax.experimental.pallas import tpu as pltpu
from jax.sharding import PartitionSpec as P

R = 128
MESH = pl.DeviceIdType.MESH
CHUNKS = (1280, 1280, 1024, 512)
STEP = 16
TILE = 256
NZ, NX, NC, NY = 8, 4, 2, 4
XY = [(dx, dy) for dy in range(NY) for dx in range(NX) if dx or dy]


def hops(step):
    return min(step[0], NX - step[0]) + min(step[1], NY - step[1])


XY.sort(key=hops)
ROW = [(dx, dc) for dx in (0, 2, 1, 3) for dc in range(NC) if dx or dc]


def far_first(size):
    return sorted(range(1, size), key=lambda k: -min(k, size - k))


def split(value):
    high = value.astype(jnp.bfloat16)
    low = (value - high.astype(jnp.float32)).astype(jnp.bfloat16)
    return high, low


def dot_rows(left, right):
    return lax.dot_general(left, right, (((0,), (0,)), ((), ())), preferred_element_type=jnp.float32)


def gather_kernel(basis_hbm, snaps_hbm, out, basis, snaps, part, from_x, from_z, block,
                  in_sem, x_send, x_recv, z_send, z_recv, xy_send, xy_recv,
                  f_send, f_recv, own_sem):
    pts, y = lax.axis_index("pts"), lax.axis_index("snap")
    z, x, c = pts // (NX * NC), (pts // NC) % NX, pts % NC
    quarter = part.shape[2]
    ends = [sum(CHUNKS[:k + 1]) for k in range(len(CHUNKS))]
    spans = [pl.ds(end - rows, rows) for end, rows in zip(ends, CHUNKS)]

    def device(z_of, x_of, c_of, y_of):
        return ((z_of * NX + x_of) * NC + c_of, y_of)

    sibling = device(z, x, 1 - c, y)
    z_peers = [device((z + k) % NZ, x, c, y) for k in range(1, NZ)]
    xy_peers = [device(z, (x + dx) % NX, c, (y + dy) % NY) for dx, dy in XY]
    row_peers = [device(z, (x + dx) % NX, (c + dc) % NC, y) for dx, dc in ROW]
    sends = []

    loads = []
    for k, span in enumerate(spans):
        for j, (src, dst) in enumerate(((basis_hbm, basis), (snaps_hbm, snaps))):
            load = pltpu.make_async_copy(src.at[span], dst.at[span], in_sem.at[k, j])
            load.start()
            loads.append(load)

    barrier = pltpu.get_barrier_semaphore()
    greeted = [peer for peer, (_, dc) in zip(row_peers, ROW) if dc] + z_peers + xy_peers
    for peer_id in greeted:
        pl.semaphore_signal(barrier, inc=1, device_id=peer_id, device_id_type=MESH)

    def send(src, dst, send_sem, recv_sem, target):
        copy = pltpu.make_async_remote_copy(src, dst, send_sem, recv_sem, device_id=target, device_id_type=MESH)
        copy.start()
        sends.append(copy)
        return copy

    for k, span in enumerate(spans):
        loads[2 * k].wait()
        loads[2 * k + 1].wait()
        b_high, b_low = split(basis[span])
        s_high, s_low = split(snaps[span])
        both = dot_rows(jnp.concatenate([b_high, b_low], axis=1), s_high)
        term = both[:R] + both[R:] + dot_rows(b_high, s_low)
        for h in range(NC):
            if k == 0:
                part[h] = term[:, h * R:(h + 1) * R].reshape(part.shape[1:])
            else:
                part[h] += term[:, h * R:(h + 1) * R].reshape(part.shape[1:])
    pl.semaphore_wait(barrier, len(greeted))

    copies = [send(part.at[(c + dc) % NC, (x + dx) % NX], from_x.at[n], x_send.at[n], x_recv.at[n], row_peers[n])
              for n, (dx, dc) in enumerate(ROW)]
    for copy in copies:
        copy.wait_recv()
    total = part[c, x]
    for n in range(len(ROW)):
        total += from_x[n]
    from_z[z] = total

    copies = [send(from_z.at[z], from_z.at[z], z_send.at[k - 1], z_recv.at[k - 1], z_peers[k - 1]) for k in far_first(NZ)]
    for copy in copies:
        copy.wait_recv()
    total = from_z[0]
    for k in range(1, NZ):
        total += from_z[k]
    block[...] = total

    def place(x_of, y_of):
        return out.at[NC * y_of + c, pl.ds(pl.multiple_of(x_of * quarter, quarter), quarter)]

    mine = place(x, y)
    last = len(XY)
    copies, handed = {}, []
    handed.append(send(block, mine, f_send.at[last], f_recv.at[last], sibling))
    for n in range(last - 1, -1, -1):
        copies[n] = send(block, mine, xy_send.at[n], xy_recv.at[n], xy_peers[n])
    own = pltpu.make_async_copy(block, mine, own_sem)
    own.start()
    for n in range(last):
        copies[n].wait_recv()
        dx, dy = XY[n]
        came = place((x - dx + NX) % NX, (y - dy + NY) % NY)
        handed.append(send(came, came, f_send.at[n], f_recv.at[n], sibling))
    for copy in handed:
        copy.wait_recv()
    for copy in sends:
        copy.wait_send()
    own.wait()


def gather_call(basis, snapshots):
    points, width = snapshots.shape
    dma = pltpu.SemaphoreType.DMA
    block = (NX, R // NX, R)
    return pl.pallas_call(
        gather_kernel,
        out_shape=jax.ShapeDtypeStruct((NC * NY, R + STEP, R), jnp.float32),
        in_specs=[pl.BlockSpec(memory_space=pl.ANY)] * 2,
        out_specs=pl.BlockSpec(memory_space=pl.ANY),
        scratch_shapes=[
            pltpu.VMEM((points, R), jnp.float32),
            pltpu.VMEM((points, width), jnp.float32),
            pltpu.VMEM((NC,) + block, jnp.float32),
            pltpu.VMEM((len(ROW),) + block[1:], jnp.float32),
            pltpu.VMEM((NZ,) + block[1:], jnp.float32),
            pltpu.VMEM(block[1:], jnp.float32),
            dma((len(CHUNKS), 2)),
            dma((len(ROW),)), dma((len(ROW),)),
            dma((NZ - 1,)), dma((NZ - 1,)),
            dma((len(XY),)), dma((len(XY),)),
            dma((len(XY) + 1,)), dma((len(XY) + 1,)),
            dma,
        ],
        compiler_params=pltpu.CompilerParams(collective_id=0, has_side_effects=True, vmem_limit_bytes=52 << 20),
        name="project_and_gather",
    )(basis, snapshots)


def first_index(pair):
    found = jnp.int32(0)
    for step in (64, 32, 16, 8, 4, 2, 1):
        tried = found + step
        found = jnp.where(pairs_before(tried) <= pair, tried, found)
    return found


def pairs_before(i):
    return R * i - i * (i - 1) // 2


def build_features(coords, feats, start, count):
    first, last = first_index(start), first_index(start + count - 1)

    @pl.loop(first, last + 1)
    def _(i):
        begun = pairs_before(i)
        into = jnp.maximum(begun - start, 0)
        j = i + jnp.maximum(start - begun, 0)
        length = jnp.minimum(R - j, count - into)
        base = coords[:, pl.ds(i, 1), :]

        @pl.loop(0, (length + STEP - 1) // STEP)
        def _(m):
            feats[:, pl.ds(into + m * STEP, STEP), :] = base * coords[:, pl.ds(j + m * STEP, STEP), :]


def lanes(blocks):
    return jnp.concatenate([blocks[t] for t in range(blocks.shape[0])], axis=1)


def gram_kernel(coords, reg_lin, reg_quad, local_out, quad_out, cross_out, lin_out, row_feats, col_feats, rows_split, lin_split):
    pts, y = lax.axis_index("pts"), lax.axis_index("snap")
    row_count, col_count = quad_out.shape
    padded = rows_split.shape[1]
    total = rows_split.shape[2]
    scale = 1.0 / total
    row_start, col_start = pts * row_count, y * col_count
    for h in range(NC):
        local_out[:, h * R:(h + 1) * R] = coords[NC * y + h, :R, :]
    build_features(coords, row_feats, row_start, row_count)
    build_features(coords, col_feats, col_start, col_count)

    for t in range(coords.shape[0]):
        high, low = split(row_feats[t, :padded, :])
        rows_split[0, :, t * R:(t + 1) * R] = high
        rows_split[1, :, t * R:(t + 1) * R] = low
        extra = jnp.where(lax.broadcasted_iota(jnp.int32, (padded - R, R), 0) == 0, 1.0, 0.0)
        high, low = split(jnp.concatenate([coords[t, :R, :], extra], axis=0))
        lin_split[0, :, t * R:(t + 1) * R] = high
        lin_split[1, :, t * R:(t + 1) * R] = low

    def product(left, right_high, right_low):
        dims = (((1,), (1,)), ((), ()))
        both = lax.dot_general(left[...].reshape(2 * padded, total), right_high, dims, preferred_element_type=jnp.float32)
        return both[:padded] + both[padded:] + lax.dot_general(left[0], right_low, dims, preferred_element_type=jnp.float32)

    def regs_down(reg):
        shape = (padded, reg.shape[1])
        on = lax.broadcasted_iota(jnp.int32, shape, 0) == lax.broadcasted_iota(jnp.int32, shape, 1)
        return on, jnp.sum(jnp.where(on, jnp.broadcast_to(reg[...], shape), 0.0), axis=1, keepdims=True)

    on, reg_column = regs_down(reg_lin)
    size = lin_out.shape[0]
    cross_out[...] = (product(lin_split, rows_split[0], rows_split[1]) * scale)[:size, :row_count]
    gram = (product(lin_split, lin_split[0], lin_split[1]) * scale)[:size, :size]
    lin_out[...] = gram + jnp.where(on[:size, :size], reg_column[:size], 0.0)

    _, reg_column = regs_down(reg_quad)

    def tile(begin, width, kept):
        feats = [split(col_feats[t, pl.ds(begin, width), :]) for t in range(coords.shape[0])]
        gram = product(rows_split, jnp.concatenate([f[0] for f in feats], axis=1), jnp.concatenate([f[1] for f in feats], axis=1)) * scale
        shape = gram.shape
        on_diag = (lax.broadcasted_iota(jnp.int32, shape, 1) - lax.broadcasted_iota(jnp.int32, shape, 0)
                   == row_start - col_start - begin)
        gram += jnp.where(on_diag, reg_column, 0.0)
        quad_out[:, pl.ds(begin, kept)] = gram[:row_count, :kept]

    whole = col_count // TILE

    @pl.loop(0, whole, unroll=8)
    def _(n):
        tile(pl.multiple_of(n * TILE, TILE), TILE, TILE)

    if col_count > whole * TILE:
        tile(whole * TILE, R, col_count - whole * TILE)


def up(value, multiple):
    return -(-value // multiple) * multiple


def gram_call(coords, reg_linear, reg_quadratic, quad_count):
    chunks, _, width = coords.shape
    total = chunks * width
    row_count, col_count = reg_quadratic.shape[0], quad_count // NY
    size = reg_linear.shape[0]
    padded = up(row_count, 16)
    vmem = pl.BlockSpec(memory_space=pltpu.VMEM)
    f32 = jnp.float32
    return pl.pallas_call(
        gram_kernel,
        out_shape=(
            jax.ShapeDtypeStruct((R, NC * R), f32),
            jax.ShapeDtypeStruct((row_count, col_count), f32),
            jax.ShapeDtypeStruct((size, row_count), f32),
            jax.ShapeDtypeStruct((size, size), f32),
        ),
        in_specs=[vmem] * 3,
        out_specs=(vmem,) * 4,
        scratch_shapes=[
            pltpu.VMEM((chunks, up(row_count, STEP) + STEP, width), f32),
            pltpu.VMEM((chunks, up(col_count, R) + STEP, width), f32),
            pltpu.VMEM((2, padded, total), jnp.bfloat16),
            pltpu.VMEM((2, padded, total), jnp.bfloat16),
        ],
        compiler_params=pltpu.CompilerParams(vmem_limit_bytes=48 << 20),
        name="pair_gram",
    )(coords, reg_linear.reshape(1, -1), reg_quadratic.reshape(1, -1))


def shards(snapshots, basis, reg_linear, reg_quadratic):
    coords = gather_call(basis, snapshots)
    return gram_call(coords, reg_linear, reg_quadratic, reg_quadratic.shape[0] * NZ * NX * NC)


def solution(mesh):
    placed = (P("pts", "snap"), P("pts", None), P(), P("pts"))
    return jax.shard_map(
        shards,
        mesh=mesh,
        in_specs=placed,
        out_specs=(P(None, "snap"), P("pts", "snap"), P(None, "pts"), P()),
        check_vma=False,
    )
```
